256 devices in a mesh: blk: 16 (over y_hi, x, core), batch: 16 (over z, y_lo).
Axes of the slice: x: 4, y: 4 (y_hi: 2, y_lo: 2; y = y_hi * 2 + y_lo), z: 8, core: 2. Of those that a mesh axis runs over, the one named last changes fastest.
Arguments:
- tokens: bfloat16 [1024, 10240], P('batch', 'blk'), may hold values from -6 to 6
- gain: bfloat16 [10240], P('blk'), may hold values from 0.099609375 to 1.8984375
- wq: bfloat16 [10240, 12288], P('blk', 'batch'), may hold values from -16 to 16
- wkv: bfloat16 [10240, 512], P('blk'), may hold values from -1 to 1
- w_gate: bfloat16 [10240, 36864], P('blk', 'batch'), may hold values from -0.0625 to 0.0625
- w_up: bfloat16 [10240, 36864], P('blk', 'batch'), may hold values from -0.0625 to 0.0625
- wo: bfloat16 [12288, 10240], P('batch', 'blk'), may hold values from -0.0546875 to 0.0546875
- w_down: bfloat16 [36864, 10240], P('batch', 'blk'), may hold values from -0.03125 to 0.03125
Outputs:
- mixed: float32 [1024, 10240], P('batch', 'blk')
The draws below stay inside these ranges and needn't reach their ends.
All inputs are finite; a program needn't handle non-finite values.
Results may differ from the reference program's by a relative error of at most 0.025.
Values may be sent and summed in bfloat16 or wider, within the bound.
No kernel may reach another device: no remote copies, remote signals or barrier semaphores. Data moves between devices by JAX's collectives and lax.ppermute only.
A program may use at most 128 MiB of HBM per device.

```python
import math
import jax
import jax.numpy as jnp
from jax import lax

D = 10240
H = 48
DH = 256
FF = 36864
LEN = 1024
N_BLK = 16


def shared_keys(key):
    return jnp.clip(jax.random.normal(key, (D, DH), jnp.float32), -6.0, 6.0) * D ** (-0.5)


def draw_wkv(key, part):
    key_part = shared_keys(key)
    key = jax.random.fold_in(key, 5)
    value_part = jnp.clip(jax.random.normal(key, (D, DH), jnp.float32), -6.0, 6.0) * D ** (-0.5)
    return jnp.concatenate([key_part, value_part], axis=1).astype(jnp.bfloat16)


def draw_wq(key, part):
    key = jax.random.fold_in(key, 7)
    noise_key = jax.random.fold_in(key, 0)
    noise = jnp.clip(jax.random.normal(noise_key, (D, H * DH), jnp.float32), -6.0, 6.0) * D ** (-0.5)
    return noise.astype(jnp.bfloat16)


def shard_levels(rng, extent, cuts, smallest, largest):
    loudness, own = 1.0, jax.random.fold_in(rng, 6)
    for axis_at, shards_of in cuts:
        draws = jnp.exp(jax.random.uniform(jax.random.fold_in(own, axis_at), (shards_of,), jnp.float32, smallest / len(cuts), largest / len(cuts)))
        loudness = loudness * jnp.repeat(draws, extent[axis_at] // shards_of).reshape([-1 if axis == axis_at else 1 for axis in range(len(extent))])
    return loudness


def centred(rng, shape, scale, bound, shards=(), held_as=jnp.bfloat16):
    result = scale * jax.random.normal(rng, shape, jnp.float32)
    if shards:
        result = result * shard_levels(rng, shape, shards, -0.22, 0.18)
    return jnp.clip(result, -bound, bound).astype(held_as)


def setup_inputs(seed: int = 0) -> dict:
    splits = jax.random.split(jax.random.key(seed), 9)
    tokens = centred(splits[0], (LEN, D), 1.0, 6.0, ((0, 16), (1, 16)))
    gain = jnp.clip(1.0 + 0.18 * jax.random.normal(splits[1], (D,), jnp.float32), 0.099609375, 1.8984375).astype(jnp.bfloat16)
    wq = draw_wq(jax.random.fold_in(splits[8], 71), 0)
    wkv = draw_wkv(jax.random.fold_in(splits[8], 71), 0)
    w_gate = centred(splits[4], (D, FF), D ** -0.5, 0.0625, ((0, 16), (1, 16)))
    w_up = centred(splits[5], (D, FF), D ** -0.5, 0.0625, ((0, 16), (1, 16)))
    wo = centred(splits[6], (H * DH, D), (H * DH) ** -0.5, 0.0546875, ((0, 16), (1, 16)))
    w_down = centred(splits[7], (FF, D), FF ** -0.5, 0.03125, ((0, 16), (1, 16)))
    return {"tokens": tokens, "gain": gain, "wq": wq, "wkv": wkv, "w_gate": w_gate, "w_up": w_up, "wo": wo, "w_down": w_down}


def rotate(tensor, positions):
    half = tensor.shape[-1] // 2
    freq = jnp.exp(jnp.arange(half).astype(jnp.float32) * (-math.log(10000.0) / half))
    angle = positions[..., None] * freq
    cosine = jnp.cos(angle)
    sine = jnp.sin(angle)
    first_half = tensor[..., :half]
    second_half = tensor[..., half:]
    return jnp.concatenate([first_half * cosine - second_half * sine, first_half * sine + second_half * cosine], axis=-1)

def reference(tokens, gain, wq, wkv, w_gate, w_up, wo, w_down):
    tokens_f = tokens.astype(jnp.float32)
    row_scale = lax.rsqrt(lax.optimization_barrier(jnp.mean(tokens_f * tokens_f, axis=1)) + 1e-06)
    scaled = (tokens_f * gain.astype(jnp.float32)).astype(jnp.bfloat16)
    width = D // N_BLK

    def add_group(carry, group_index):
        offset = (group_index * width).astype(jnp.int32)
        columns = lax.dynamic_slice_in_dim(scaled, offset, width, 1)
        updated = []
        for partial_sum, matrix in zip(carry, (wq, w_gate, w_up)):
            weight_rows = lax.dynamic_slice_in_dim(matrix, offset, width, 0)
            term = jnp.dot(columns, weight_rows, preferred_element_type=jnp.float32).astype(jnp.bfloat16)
            term = lax.optimization_barrier(term).astype(jnp.float32)
            updated.append(partial_sum + term)
        return (tuple(updated), None)
    start_sums = (jnp.zeros((LEN, H * DH), jnp.float32), jnp.zeros((LEN, FF), jnp.float32), jnp.zeros((LEN, FF), jnp.float32))
    (q_sum, g_sum, u_sum), unused = lax.scan(add_group, start_sums, jnp.arange(N_BLK).astype(jnp.int32))
    kv_sum = jnp.dot(scaled, wkv, preferred_element_type=jnp.float32)
    positions = jnp.arange(LEN).astype(jnp.float32)
    scale_col = row_scale[:, None]
    key_rows = rotate(scale_col * kv_sum[:, :DH], positions).astype(jnp.bfloat16)
    value_rows = (scale_col * kv_sum[:, DH:]).astype(jnp.bfloat16)
    queries = rotate((scale_col * q_sum).reshape(LEN, H, DH), positions[:, None]).astype(jnp.bfloat16)
    hidden = (jax.nn.silu(scale_col * g_sum) * (scale_col * u_sum)).astype(jnp.bfloat16)
    scores = jnp.einsum('qhd,kd->hqk', queries.astype(jnp.float32), key_rows.astype(jnp.float32)) * float(DH) ** (-0.5)
    order = jnp.arange(LEN)
    allowed = order[:, None] >= order[None, :]
    scores = jnp.where(allowed[None], scores, -1e+30)
    top_score = lax.optimization_barrier(jnp.max(scores, axis=-1, keepdims=True))
    expo = jnp.exp(scores - top_score)
    weights = (expo / lax.optimization_barrier(jnp.sum(expo, axis=-1, keepdims=True))).astype(jnp.bfloat16)
    attended = jnp.einsum('hqk,kd->qhd', weights.astype(jnp.float32), value_rows.astype(jnp.float32))
    attended = attended.astype(jnp.bfloat16).reshape(LEN, H * DH)
    summed_out = jnp.dot(attended, wo, preferred_element_type=jnp.float32) + jnp.dot(hidden, w_down, preferred_element_type=jnp.float32)
    return (tokens_f + summed_out).astype(jnp.float32)
```

```python
import math

import jax
import jax.numpy as jnp
from jax import lax
from jax.sharding import PartitionSpec as P

BF = jnp.bfloat16
F32 = jnp.float32
STAGES = ((0, 1, 7, 2), (6, 3, 5, 4))


def blk_perm(dyh, dx, dc):
    pairs = []
    for b in range(16):
        yh, x, c = b // 8, (b // 2) % 4, b % 2
        pairs.append((b, ((yh + dyh) % 2) * 8 + ((x + dx) % 4) * 2 + (c + dc) % 2))
    return pairs


def blk_send(value, dyh=0, dx=0, dc=0):
    return lax.ppermute(value, "blk", blk_perm(dyh, dx, dc))


def blk_send_xor(value, xor):
    pairs = []
    for b in range(16):
        yh, x, c = b // 8, (b // 2) % 4, b % 2
        pairs.append((b, yh * 8 + (x ^ xor) * 2 + c))
    return lax.ppermute(value, "blk", pairs)


def bat_send(value, dz=0, dyl=0):
    pairs = [(t, ((t // 2 + dz) % 8) * 2 + (t + dyl) % 2) for t in range(16)]
    return lax.ppermute(value, "batch", pairs)


def roll_lead(value, shift, axis):
    n = value.shape[axis]
    return lax.dynamic_slice_in_dim(
        jnp.concatenate([value, value], axis=axis), shift, n, axis
    )


def flip_if(value, flag, axis):
    first = lax.slice_in_dim(value, 0, 1, axis=axis)
    second = lax.slice_in_dim(value, 1, 2, axis=axis)
    return jnp.where(flag, jnp.concatenate([second, first], axis=axis), value)


def rotate(tensor, positions):
    half = tensor.shape[-1] // 2
    freq = jnp.exp(jnp.arange(half).astype(F32) * (-math.log(10000.0) / half))
    angle = positions[..., None] * freq
    cosine = jnp.cos(angle)
    sine = jnp.sin(angle)
    first_half = tensor[..., :half]
    second_half = tensor[..., half:]
    return jnp.concatenate(
        [first_half * cosine - second_half * sine, first_half * sine + second_half * cosine],
        axis=-1,
    )


def on_device(tokens, gain, wq, wkv, w_gate, w_up, wo, w_down):
    b = lax.axis_index("blk")
    t = lax.axis_index("batch")
    yh, x, c = b // 8, (b // 2) % 4, b % 2
    z, yl = t // 2, t % 2
    rows, width = tokens.shape
    features = width * 16
    nq, nh = wq.shape[1], w_gate.shape[1]
    head = wkv.shape[1] // 2
    heads = nq // head
    half_rows = rows // 2

    tokens_f = tokens.astype(F32)
    scaled = (tokens_f * gain.astype(F32)).astype(BF)

    pair = jnp.concatenate([scaled, bat_send(scaled, dyl=1)], axis=0)
    by_z = {0: pair}
    for stage in STAGES:
        for d in stage:
            if d:
                by_z[d] = bat_send(pair, dz=-d)

    squares = jnp.sum(tokens_f * tokens_f, axis=1, keepdims=True)
    kv_part = jnp.dot(scaled, wkv, preferred_element_type=F32)
    payload = jnp.concatenate([kv_part, jnp.broadcast_to(squares, (rows, 128))], axis=1)
    payload = flip_if(payload.reshape(2, half_rows, -1), c == 1, 0)
    kv_sum = payload[0] + blk_send(payload[1], dc=1)
    kv_sum = kv_sum + blk_send_xor(kv_sum, 1)
    kv_sum = kv_sum + blk_send_xor(kv_sum, 2)
    kv_sum = kv_sum + blk_send(kv_sum, dyh=1)
    row_scale = lax.rsqrt(kv_sum[:, 2 * head : 2 * head + 1] / features + 1e-06)
    own_positions = (t * rows + c * half_rows + jnp.arange(half_rows)).astype(F32)
    key_own = rotate(row_scale * kv_sum[:, :head], own_positions).astype(BF)
    value_own = (row_scale * kv_sum[:, head : 2 * head]).astype(BF)
    scale_hi = lax.reduce_precision(row_scale, 8, 7)
    scale_mid = lax.reduce_precision(row_scale - scale_hi, 8, 7)
    scale_lo = row_scale - scale_hi - scale_mid
    lane = lax.broadcasted_iota(jnp.int32, (half_rows, 128), 1)
    scale_cols = jnp.where(
        lane == 0, scale_hi, jnp.where(lane == 1, scale_mid, jnp.where(lane == 2, scale_lo, 0.0))
    ).astype(BF)
    kv_own = jnp.concatenate([key_own, value_own, scale_cols], axis=1)
    kv_half = lax.all_to_all(
        jnp.broadcast_to(kv_own[None], (16,) + kv_own.shape), "batch", 0, 0
    )
    kv_other = blk_send(kv_half, dc=1)
    kv_all = flip_if(jnp.stack([kv_half, kv_other], axis=1), c == 1, 1)
    kv_all = kv_all.reshape(16 * rows, -1)
    seq = 16 * rows
    key_rows = kv_all[:, :head]
    value_rows = kv_all[:, head : 2 * head]
    scale_pack = kv_all[:, 2 * head :]

    out_sum = tokens_f
    for stage in STAGES:
        count = len(stage) * 2 * rows
        r = count // 16
        tok = jnp.concatenate([by_z[d] for d in stage], axis=0).reshape(2, 4, 2, r, width)
        tok = roll_lead(flip_if(flip_if(tok, c == 1, 0), yh == 1, 2), x, 1)
        far, near = tok[1].reshape(8 * r, width), tok[0].reshape(8 * r, width)

        def project(part):
            return jnp.concatenate(
                [
                    jnp.dot(part, w, preferred_element_type=F32).astype(BF)
                    for w in (wq, w_gate, w_up)
                ],
                axis=1,
            )

        sent = blk_send(project(far), dc=1)
        s1 = (project(near).astype(F32) + sent.astype(F32)).astype(BF)
        s1 = s1.reshape(8, r, -1)
        from_left = blk_send(s1[3:5], dx=1)
        from_right = blk_send(s1[5:7], dx=-1)
        up_sum = (s1[2].astype(F32) + from_left[1].astype(F32)).astype(BF)
        down_sum = (s1[7].astype(F32) + from_right[0].astype(F32)).astype(BF)
        left_sum = blk_send(up_sum, dx=1)
        right_sum = blk_send(down_sum, dx=-1)
        s2_far = (
            s1[1].astype(F32) + from_left[0].astype(F32) + right_sum.astype(F32)
        ).astype(BF)
        s2_near = s1[0].astype(F32) + from_right[1].astype(F32) + left_sum.astype(F32)
        summed = s2_near + blk_send(s2_far, dyh=1).astype(F32)

        index = (c * 8 + x * 2 + yh) * r + jnp.arange(r)
        shift = sum(
            jnp.where(index // (2 * rows) == k, d, 0) for k, d in enumerate(stage)
        )
        chunk = ((z + shift) % 8) * 2 + (yl + index // rows) % 2
        positions = chunk * rows + index % rows
        onehot = (positions[:, None] == jnp.arange(seq)[None, :]).astype(BF)
        scale = jnp.sum(
            jnp.dot(onehot, scale_pack, preferred_element_type=F32)[:, :3], axis=1, keepdims=True
        )
        queries = (scale * summed[:, :nq]).reshape(r, heads, head)
        queries = rotate(queries, positions.astype(F32)[:, None]).astype(BF)
        hidden = (
            jax.nn.silu(scale * summed[:, nq : nq + nh]) * (scale * summed[:, nq + nh :])
        ).astype(BF)
        scores = jnp.einsum(
            "qhd,kd->hqk", queries, key_rows, preferred_element_type=F32
        ) * float(head) ** (-0.5)
        allowed = positions[:, None] >= jnp.arange(seq)[None, :]
        scores = jnp.where(allowed[None], scores, -1e30)
        top_score = jnp.max(scores, axis=-1, keepdims=True)
        expo = jnp.exp(scores - top_score)
        weights = (expo / jnp.sum(expo, axis=-1, keepdims=True)).astype(BF)
        attended = jnp.einsum("hqk,kd->qhd", weights, value_rows, preferred_element_type=F32)
        attended = attended.astype(BF).reshape(r, nq)
        branch = jnp.concatenate([attended, hidden], axis=1)

        both = jnp.stack([branch, blk_send(branch, dyh=1)], axis=0)
        right = blk_send(both, dx=-1)
        left = blk_send(both, dx=1)
        across_0 = blk_send(right[0], dx=-1)
        across_1 = blk_send(left[1], dx=1)
        mine = jnp.concatenate(
            [both, right, across_0[None], across_1[None], left], axis=0
        ).reshape(8 * r, nq + nh)
        theirs = blk_send(mine, dc=1)

        def project_out(part):
            return jnp.dot(part[:, :nq], wo, preferred_element_type=F32) + jnp.dot(
                part[:, nq:], w_down, preferred_element_type=F32
            )

        out = jnp.stack([project_out(mine), project_out(theirs)], axis=0)
        out = out.reshape(2, 4, 2, r, width)
        out = roll_lead(flip_if(flip_if(out, c == 1, 0), yh == 1, 2), (4 - x) % 4, 1)
        out = out.reshape(len(stage), 2, rows, width)
        out = out[:, 0] + bat_send(out[:, 1].astype(BF), dyl=1).astype(F32)
        for k, d in enumerate(stage):
            part = out[k]
            if d:
                part = bat_send(part.astype(BF), dz=d).astype(F32)
            out_sum = out_sum + part
    return out_sum


def solution(mesh):
    in_specs = (
        P("batch", "blk"),
        P("blk"),
        P("blk", "batch"),
        P("blk", None),
        P("blk", "batch"),
        P("blk", "batch"),
        P("batch", "blk"),
        P("batch", "blk"),
    )
    out_specs = P("batch", "blk")
    return jax.shard_map(
        on_device, mesh=mesh, in_specs=in_specs, out_specs=out_specs, check_vma=False
    )
```

```python
import math

import jax
import jax.numpy as jnp
from jax import lax
from jax.experimental import pallas as pl
from jax.experimental.pallas import tpu as pltpu
from jax.sharding import PartitionSpec as P

BF = jnp.bfloat16
F32 = jnp.float32
STAGES = (32, 32)
Z_GROUPS = [[2 * z + yl for z in range(8)] for yl in range(2)]
NO_COST = pl.CostEstimate(flops=1, bytes_accessed=1, transcendentals=0)


def cost(microseconds):
    return pl.CostEstimate(
        flops=int(microseconds * 1.15e9), bytes_accessed=1, transcendentals=0
    )


BIG = 58 * 2**20


def blk_send(value, dyh=0, dx=0, dc=0, xor=0):
    pairs = []
    for b in range(16):
        yh, x, c = b // 8, (b // 2) % 4, b % 2
        to_x = ((x ^ xor) + dx) % 4
        pairs.append((b, ((yh + dyh) % 2) * 8 + to_x * 2 + (c + dc) % 2))
    return lax.ppermute(value, "blk", pairs)


def angles(positions, half):
    freq = jnp.exp(jnp.arange(half).astype(F32) * (-math.log(10000.0) / half))
    angle = positions.astype(F32)[:, None] * freq
    return jnp.cos(angle), jnp.sin(angle)


def turn(tensor, cosine, sine):
    half = tensor.shape[-1] // 2
    first, second = tensor[:, :half], tensor[:, half:]
    return jnp.concatenate(
        [first * cosine - second * sine, first * sine + second * cosine], axis=-1
    )


def whole(count):
    return [pl.BlockSpec(memory_space=pltpu.VMEM)] * count


def after(deps):
    return [pl.BlockSpec(memory_space=pl.ANY)] * len(deps)


def simple_call(body, out_shape, operands, deps, name, time=1.2):
    count = len(operands)

    def kernel(*refs):
        body(*refs[:count], *refs[count + len(deps) :])

    return pl.pallas_call(
        kernel,
        in_specs=whole(count) + after(deps),
        out_specs=jax.tree.map(lambda _: pl.BlockSpec(memory_space=pltpu.VMEM), out_shape),
        out_shape=out_shape,
        compiler_params=pltpu.CompilerParams(vmem_limit_bytes=20 * 2**20),
        cost_estimate=cost(time),
        name=name,
    )(*operands, *deps)


def project(place, toks, wqs, gates, ups, deps, name):
    chunks, rows_each, width = toks[0].shape
    count = chunks * rows_each
    group = count // 4
    part = group // 2
    each = chunks // 4
    tile = wqs[0].shape[1] // 2
    half = gates[1].shape[1]

    def kernel(place_ref, t0, t1, q0, q1, g0, g1, u0, u1, *rest):
        low_ref, up_ref, top_ref, right_ref, left_ref, rows0, rows1 = rest[len(deps) :]
        j = pl.program_id(0)

        def store(at, value):
            columns = slice(at, at + value.shape[1])
            low_ref[:, columns] = value[0 : 2 * part]
            up_ref[:, columns] = value[2 * part : 3 * part]
            right_ref[:, columns] = value[3 * part : 5 * part]
            left_ref[:, columns] = value[5 * part : 7 * part]
            top_ref[:, columns] = value[7 * part : 8 * part]

        def finish(at, w0, w1):
            term = jnp.dot(rows0[...], w0[...], preferred_element_type=F32)
            term = term + jnp.dot(rows1[...], w1[...], preferred_element_type=F32)
            store(at, term.astype(BF))

        @pl.when(j == 0)
        def _():
            for k in range(4):
                at = lax.rem(place_ref[1] + k, 4) * each
                own = slice(k * group, (k + 1) * group)
                rows0[own, :] = t0[pl.ds(at, each)].reshape(group, width)
                rows1[own, :] = t1[pl.ds(at, each)].reshape(group, width)
            starts = [pl.multiple_of(k * group + place_ref[0] * part, part) for k in range(4)]
            left = jnp.concatenate([rows0[pl.ds(at, part), :] for at in starts], axis=0)
            right = jnp.concatenate([rows1[pl.ds(at, part), :] for at in starts], axis=0)
            term = jnp.dot(left, q0[...], preferred_element_type=F32)
            term = (term + jnp.dot(right, q1[...], preferred_element_type=F32)).astype(BF)
            pieces = []
            for k in range(4):
                own = term[k * part : (k + 1) * part]
                pieces += [own[:, :tile], own[:, tile:]]
            store(0, jnp.concatenate(pieces, axis=0))

        @pl.when(j == 1)
        def _():
            finish(tile, g0, g1)

        @pl.when(j == 2)
        def _():
            finish(tile + half, u0, u1)

    def fixed(shape):
        return pl.BlockSpec(shape, lambda j, place_ref: (0, 0))

    own_half = pl.BlockSpec((width, half), lambda j, place_ref: (0, place_ref[0]))
    taken = pl.BlockSpec((chunks, rows_each, width), lambda j, place_ref: (0, 0, 0))
    in_specs = [
        taken,
        taken,
        fixed((width, 2 * tile)),
        fixed((width, 2 * tile)),
        own_half,
        fixed((width, half)),
        own_half,
        fixed((width, half)),
    ]
    return pl.pallas_call(
        kernel,
        grid_spec=pltpu.PrefetchScalarGridSpec(
            num_scalar_prefetch=1,
            grid=(3,),
            in_specs=in_specs + after(deps),
            out_specs=[fixed((n * part, tile + 2 * half)) for n in (2, 1, 1, 2, 2)],
            scratch_shapes=[pltpu.VMEM((count, width), BF)] * 2,
        ),
        out_shape=[jax.ShapeDtypeStruct((n * part, tile + 2 * half), BF) for n in (2, 1, 1, 2, 2)],
        compiler_params=pltpu.CompilerParams(
            dimension_semantics=("arbitrary",), vmem_limit_bytes=BIG
        ),
        cost_estimate=cost(11),
        name=name,
    )(place, *toks, *wqs, *gates, *ups, *deps)


def middle(bottom, top, from_left, from_right, deps, name):
    r, whole_width = top.shape

    def body(bottom_ref, top_ref, left_ref, right_ref, up_ref, down_ref):
        up_ref[...] = (
            bottom_ref[...].astype(F32) + left_ref[r : 2 * r].astype(F32)
        ).astype(BF)
        down_ref[...] = (top_ref[...].astype(F32) + right_ref[0:r].astype(F32)).astype(BF)

    shape = jax.ShapeDtypeStruct((r, whole_width), BF)
    return simple_call(body, [shape, shape], [bottom, top, from_left, from_right], deps, name)


def tail(low, from_left, from_right, left_sum, right_sum, deps, name):
    r, whole_width = left_sum.shape

    def body(low_ref, left_ref, right_ref, ls_ref, rs_ref, out_ref):
        out_ref[0:r] = (
            low_ref[0:r].astype(F32) + right_ref[r : 2 * r].astype(F32) + ls_ref[...].astype(F32)
        ).astype(BF)
        out_ref[r : 2 * r] = (
            low_ref[r : 2 * r].astype(F32) + left_ref[0:r].astype(F32) + rs_ref[...].astype(F32)
        ).astype(BF)

    shape = jax.ShapeDtypeStruct((2 * r, whole_width), BF)
    return simple_call(
        body, shape, [low, from_left, from_right, left_sum, right_sum], deps, name
    )


def gate_all(values, deps):
    count = len(values)

    def kernel(*refs):
        pass

    return pl.pallas_call(
        kernel,
        in_specs=after(values) + after(deps),
        out_specs=after(values),
        out_shape=[jax.ShapeDtypeStruct(value.shape, value.dtype) for value in values],
        input_output_aliases={k: k for k in range(count)},
        cost_estimate=NO_COST,
        name="gate",
    )(*values, *deps)


def gate(value, deps):
    return gate_all([value], deps)[0]


def branches(own, other, kv_one, kv_two, key_pos, pos, query_pos, cosine, sine, deps, name):
    rows, total = own.shape
    part = rows // 2
    head = 2 * cosine.shape[1]
    tile = 3 * head // 2
    heads = 2 * tile // head
    each = (total // tile - 1) // 2

    def body(own_ref, oth_ref, one_ref, two_ref, kp_ref, pos_ref, qp_ref, cos_ref, sin_ref, out_ref):
        key_position = kp_ref[0:1, :]
        pack = jnp.concatenate([one_ref[:, 2 * head :], two_ref[:, 2 * head :]], axis=0)

        def scale_of(position):
            onehot = (position == key_position).astype(F32).astype(BF)
            parts = jnp.dot(onehot, pack, preferred_element_type=F32)
            return parts[:, 0:1] + parts[:, 1:2] + parts[:, 2:3]

        def block(k, start, size):
            at = (slice(start, start + size), slice(k * tile, (k + 1) * tile))
            return own_ref[at].astype(F32) + oth_ref[at].astype(F32)

        position = qp_ref[:, 0:1]
        raw = jnp.concatenate([block(0, 0, part), block(0, part, part)], axis=1)
        raw = scale_of(position) * raw
        cos, sin = cos_ref[...], sin_ref[...]
        queries = jnp.concatenate(
            [turn(raw[:, k * head : (k + 1) * head], cos, sin) for k in range(heads)], axis=0
        ).astype(BF)
        keys = jnp.concatenate([one_ref[:, :head], two_ref[:, :head]], axis=0)
        values = jnp.concatenate(
            [one_ref[:, head : 2 * head], two_ref[:, head : 2 * head]], axis=0
        )
        scores = lax.dot_general(
            queries, keys, (((1,), (1,)), ((), ())), preferred_element_type=F32
        ) * float(head) ** (-0.5)
        allowed = jnp.where(position >= key_position, 1.0, 0.0)
        allowed = jnp.concatenate([allowed] * heads, axis=0)
        scores = jnp.where(allowed > 0.5, scores, -1e30)
        expo = jnp.exp(scores - jnp.max(scores, axis=1, keepdims=True))
        weights = (expo / jnp.sum(expo, axis=1, keepdims=True)).astype(BF)
        attended = jnp.dot(weights, values, preferred_element_type=F32)
        attended = jnp.concatenate(
            [attended[k * part : (k + 1) * part] for k in range(heads)], axis=1
        ).astype(BF)
        out_ref[0:part, 0:tile] = attended[:, :tile]
        out_ref[part:rows, 0:tile] = attended[:, tile:]
        scale = scale_of(pos_ref[:, 0:1])
        for k in range(1, each + 1):
            gate_part = scale * block(k, 0, rows)
            up_part = scale * block(each + k, 0, rows)
            out_ref[:, k * tile : (k + 1) * tile] = (
                gate_part / (1.0 + jnp.exp(-gate_part)) * up_part
            ).astype(BF)

    return simple_call(
        body,
        jax.ShapeDtypeStruct((rows, (each + 1) * tile), BF),
        [own, other, kv_one, kv_two, key_pos, pos, query_pos, cosine, sine],
        deps,
        name,
        3,
    )


def project_out(place, mine, theirs, wo, w_down, deps, name, time):
    group, depth = mine[0].shape
    count = 4 * group
    part = group // 2
    width = wo.shape[1]
    tile = wo.shape[0] // 2
    half = depth - tile
    each = group // 4

    def kernel(place_ref, *refs):
        m_refs, t_refs, (wo_ref, wd_ref) = refs[0:4], refs[4:8], refs[8:10]
        keep_ref, give_ref, total, attended, hidden = refs[10 + len(deps) :]
        k = pl.program_id(0)

        @pl.when(k == 0)
        def _():
            for refs_of, core in ((m_refs, place_ref[0]), (t_refs, 1 - place_ref[0])):
                for g, ref in enumerate(refs_of):
                    at = pl.multiple_of(g * group + core * part, part)
                    for side in range(2):
                        attended[pl.ds(at, part), side * tile : (side + 1) * tile] = ref[
                            side * part : (side + 1) * part, 0:tile
                        ]
            for g, ref in enumerate(m_refs):
                hidden[g * group : (g + 1) * group, :] = ref[:, tile:]
            total[...] = jnp.dot(attended[...], wo_ref[...], preferred_element_type=F32)

        @pl.when(k == 1)
        def _():
            total[...] += jnp.dot(hidden[...], wd_ref[...], preferred_element_type=F32)
            for g, ref in enumerate(t_refs):
                hidden[g * group : (g + 1) * group, :] = ref[:, tile:]

        @pl.when(k == 2)
        def _():
            total[...] += jnp.dot(hidden[...], wd_ref[...], preferred_element_type=F32)
            mine_yl = place_ref[2]
            for g in range(4):
                for side in range(2):
                    at = lax.rem(place_ref[1] + g, 4) * 2 + side
                    start = g * group + side * 2 * each
                    own = pl.ds(pl.multiple_of(start + mine_yl * each, each), each)
                    other = pl.ds(pl.multiple_of(start + (1 - mine_yl) * each, each), each)
                    keep_ref[at] = total[own, :]
                    give_ref[at] = total[other, :].astype(BF)

    def fixed(shape):
        return pl.BlockSpec(shape, lambda k, place_ref: (0, 0))

    def down_at(k, place_ref):
        return (jnp.where(k < 2, place_ref[0], 1 - place_ref[0]), 0)

    return pl.pallas_call(
        kernel,
        grid_spec=pltpu.PrefetchScalarGridSpec(
            num_scalar_prefetch=1,
            grid=(3,),
            in_specs=[
                *[fixed((group, depth))] * 8,
                fixed((2 * tile, width)),
                pl.BlockSpec((half, width), down_at),
            ]
            + after(deps),
            out_specs=[pl.BlockSpec((8, each, width), lambda k, place_ref: (0, 0, 0))] * 2,
            scratch_shapes=[
                pltpu.VMEM((count, width), F32),
                pltpu.VMEM((count, 2 * tile), BF),
                pltpu.VMEM((count, half), BF),
            ],
        ),
        out_shape=[jax.ShapeDtypeStruct((8, each, width), kind) for kind in (F32, BF)],
        compiler_params=pltpu.CompilerParams(
            dimension_semantics=("arbitrary",), vmem_limit_bytes=BIG
        ),
        cost_estimate=cost(time),
        name=name,
    )(place, *mine, *theirs, wo, w_down, *deps)


def on_device(tokens, gain, wq, wkv, w_gate, w_up, wo, w_down):
    b = lax.axis_index("blk")
    t = lax.axis_index("batch")
    x, c = (b // 2) % 4, b % 2
    place = jnp.stack([c, x, t % 2]).astype(jnp.int32)
    rows, width = tokens.shape
    features = width * 16
    seq = rows * 16
    nq = wq.shape[1]
    head = wkv.shape[1] // 2
    half_rows = rows // 2

    tokens_f = tokens.astype(F32)
    scaled = (tokens_f * gain.astype(F32)).astype(BF)

    part = w_gate.shape[1] // 2
    wqs = (wq, blk_send(wq, dc=1))
    gates, ups = tuple(
        (w, blk_send(lax.dynamic_slice_in_dim(w, (1 - c) * part, part, 1), dc=1))
        for w in (w_gate, w_up)
    )

    starts = [sum(STAGES[:k]) for k in range(len(STAGES))]

    def spread_rows(value):
        return jnp.broadcast_to(value[None], (16,) + value.shape)

    def to_all(value):
        return lax.all_to_all(value, "batch", 0, 0)

    def position_of(k, index):
        return (index // STAGES[k]) * rows + starts[k] + index % STAGES[k]

    def wide(position):
        return jnp.broadcast_to(position[:, None], (position.shape[0], 128)).astype(jnp.int32)

    places = []
    for k, count in enumerate(STAGES):
        group = 16 * count // 4
        position = position_of(k, x * group + jnp.arange(group))
        query_at = position_of(k, x * group + c * (group // 2) + jnp.arange(group // 2))
        places.append((wide(position), wide(query_at), *angles(query_at, head // 2)))

    squares = jnp.sum(tokens_f * tokens_f, axis=1, keepdims=True)
    kv_part = jnp.dot(scaled, wkv, preferred_element_type=F32)
    payload = jnp.concatenate([kv_part, jnp.broadcast_to(squares, (rows, 128))], axis=1)
    kv_keep = lax.dynamic_slice_in_dim(payload, c * half_rows, half_rows, 0)
    kv_give = lax.dynamic_slice_in_dim(payload, (1 - c) * half_rows, half_rows, 0)
    kv_got = blk_send(kv_give, dc=1)

    kv_sum = kv_keep + kv_got
    kv_sum = kv_sum + blk_send(kv_sum, xor=1)
    kv_sum = kv_sum + blk_send(kv_sum, xor=2)

    def term_of(tok, deps):
        return project(place, (tok, blk_send(tok, dc=1)), wqs, gates, ups, deps, "term")

    def own_rows(k):
        return scaled[starts[k] : starts[k] + STAGES[k]]

    def step_one(term):
        return blk_send(term[3], dx=1), blk_send(term[4], dx=-1)

    def step_two(sums):
        return blk_send(sums[0], dx=1), blk_send(sums[1], dx=-1)

    tok_1 = gate(to_all(spread_rows(own_rows(0))), [kv_sum])
    tok_2 = to_all(gate(spread_rows(own_rows(1)), [tok_1]))
    term_1 = term_of(tok_1, [])
    one_1 = step_one(term_1)
    kv_half = gate(kv_sum, [term_1[0]])
    kv_sum = kv_half + blk_send(kv_half, dyh=1)
    tok_2 = gate(tok_2, [kv_sum])
    row_scale = lax.rsqrt(kv_sum[:, 2 * head : 2 * head + 1] / features + 1e-06)
    own_cos, own_sin = angles(t * rows + c * half_rows + jnp.arange(half_rows), head // 2)
    key_own = turn(row_scale * kv_sum[:, :head], own_cos, own_sin).astype(BF)
    value_own = (row_scale * kv_sum[:, head : 2 * head]).astype(BF)
    scale_hi = lax.reduce_precision(row_scale, 8, 7)
    scale_mid = lax.reduce_precision(row_scale - scale_hi, 8, 7)
    scale_lo = row_scale - scale_hi - scale_mid
    lane = lax.broadcasted_iota(jnp.int32, (half_rows, 128), 1)
    scale_cols = jnp.where(
        lane == 0, scale_hi, jnp.where(lane == 1, scale_mid, jnp.where(lane == 2, scale_lo, 0.0))
    ).astype(BF)
    kv_own = jnp.concatenate([key_own, value_own, scale_cols], axis=1)
    kv_own = gate(spread_rows(kv_own), [tok_2])
    mid_1 = middle(term_1[1], term_1[2], *one_1, [kv_own], "mid")
    two_1 = step_two(mid_1)
    term_2 = term_of(tok_2, [])
    one_2 = step_one(term_2)
    own_1 = tail(term_1[0], *one_1, *two_1, [], "tail")
    mid_2 = middle(term_2[1], term_2[2], *one_2, [own_1], "mid")
    two_2 = step_two(mid_2)

    kv_one = to_all(kv_own).reshape(seq // 2, -1)
    kv_two = blk_send(kv_one, dc=1)
    at = jnp.arange(seq)
    side = jnp.where(at < seq // 2, c, 1 - c)
    at = at % (seq // 2)
    key_pos = (at // half_rows) * rows + side * half_rows + at % half_rows
    key_pos = jnp.broadcast_to(key_pos[None, :], (8, seq)).astype(jnp.int32)

    def branch_of(s, own, deps, name):
        other = blk_send(own, dyh=1)
        return branches(own, other, kv_one, kv_two, key_pos, *places[s], deps, name)

    def spread(branch):
        return [blk_send(branch, dx=-k) for k in (1, 2, 3)]

    def collect(branch, others):
        mine = [branch, *others]
        return mine, [blk_send(piece, dc=1) for piece in mine]

    def pair_sum(out):
        pairs = [(k, k ^ 1) for k in range(16)]
        return (out[0] + lax.ppermute(out[1], "batch", pairs).astype(F32)).astype(BF)

    branch_1 = branch_of(0, own_1, [mid_2[0]], "branch")
    spread_1 = spread(branch_1)
    own_2 = tail(term_2[0], *one_2, *two_2, [branch_1], "tail")
    branch_2 = branch_of(1, own_2, [], "branch")
    spread_2 = spread(branch_2)
    out_1 = project_out(place, *collect(branch_1, spread_1), wo, w_down, [branch_2], "out", 8)
    spread_2 = gate_all(spread_2, [out_1[0]])
    out_2 = project_out(
        place, *collect(branch_2, spread_2), wo, w_down, [out_1[0]], "out", 8
    )
    pair = jnp.concatenate([pair_sum(out_1), pair_sum(out_2)], axis=1)
    parts = lax.all_to_all(pair, "batch", 0, 0, axis_index_groups=Z_GROUPS)
    return tokens_f + jnp.sum(parts.astype(F32), axis=0)


def solution(mesh):
    in_specs = (
        P("batch", "blk"),
        P("blk"),
        P("blk", "batch"),
        P("blk", None),
        P("blk", "batch"),
        P("blk", "batch"),
        P("batch", "blk"),
        P("batch", "blk"),
    )
    out_specs = P("batch", "blk")
    return jax.shard_map(
        on_device, mesh=mesh, in_specs=in_specs, out_specs=out_specs, check_vma=False
    )
```

```python
import math

import jax
import jax.numpy as jnp
from jax import lax
from jax.experimental import pallas as pl
from jax.experimental.pallas import tpu as pltpu
from jax.sharding import PartitionSpec as P

BF = jnp.bfloat16
F32 = jnp.float32
STAGES = (32, 32)
Z_GROUPS = [[2 * z + yl for z in range(8)] for yl in range(2)]
NO_COST = pl.CostEstimate(flops=1, bytes_accessed=1, transcendentals=0)


def cost(microseconds):
    return pl.CostEstimate(
        flops=int(microseconds * 1.15e9), bytes_accessed=1, transcendentals=0
    )


BIG = 58 * 2**20


def blk_send(value, dyh=0, dx=0, dc=0, xor=0):
    pairs = []
    for b in range(16):
        yh, x, c = b // 8, (b // 2) % 4, b % 2
        to_x = ((x ^ xor) + dx) % 4
        pairs.append((b, ((yh + dyh) % 2) * 8 + to_x * 2 + (c + dc) % 2))
    return lax.ppermute(value, "blk", pairs)


def angles(positions, half):
    freq = jnp.exp(jnp.arange(half).astype(F32) * (-math.log(10000.0) / half))
    angle = positions.astype(F32)[:, None] * freq
    return jnp.cos(angle), jnp.sin(angle)


def turn(tensor, cosine, sine):
    half = tensor.shape[-1] // 2
    first, second = tensor[:, :half], tensor[:, half:]
    return jnp.concatenate(
        [first * cosine - second * sine, first * sine + second * cosine], axis=-1
    )


def whole(count):
    return [pl.BlockSpec(memory_space=pltpu.VMEM)] * count


def after(deps):
    return [pl.BlockSpec(memory_space=pl.ANY)] * len(deps)


def simple_call(body, out_shape, operands, deps, name, time=1.2):
    count = len(operands)

    def kernel(*refs):
        body(*refs[:count], *refs[count + len(deps) :])

    return pl.pallas_call(
        kernel,
        in_specs=whole(count) + after(deps),
        out_specs=jax.tree.map(lambda _: pl.BlockSpec(memory_space=pltpu.VMEM), out_shape),
        out_shape=out_shape,
        compiler_params=pltpu.CompilerParams(vmem_limit_bytes=20 * 2**20),
        cost_estimate=cost(time),
        name=name,
    )(*operands, *deps)


def project(place, toks, wqs, gates, ups, deps, name):
    chunks, rows_each, width = toks[0].shape
    count = chunks * rows_each
    group = count // 4
    part = group // 2
    each = chunks // 4
    tile = wqs[0].shape[1] // 2
    half = gates[1].shape[1]

    def kernel(place_ref, t0, t1, q0, q1, g0, g1, u0, u1, *rest):
        low_ref, up_ref, top_ref, right_ref, left_ref, rows0, rows1 = rest[len(deps) :]
        j = pl.program_id(0)

        def store(at, value):
            columns = slice(at, at + value.shape[1])
            low_ref[:, columns] = value[0 : 2 * part]
            up_ref[:, columns] = value[2 * part : 3 * part]
            right_ref[:, columns] = value[3 * part : 5 * part]
            left_ref[:, columns] = value[5 * part : 7 * part]
            top_ref[:, columns] = value[7 * part : 8 * part]

        def finish(at, w0, w1):
            term = jnp.dot(rows0[...], w0[...], preferred_element_type=F32)
            term = term + jnp.dot(rows1[...], w1[...], preferred_element_type=F32)
            store(at, term.astype(BF))

        @pl.when(j == 0)
        def _():
            for k in range(4):
                at = lax.rem(place_ref[1] + k, 4) * each
                own = slice(k * group, (k + 1) * group)
                rows0[own, :] = t0[pl.ds(at, each)].reshape(group, width)
                rows1[own, :] = t1[pl.ds(at, each)].reshape(group, width)
            starts = [pl.multiple_of(k * group + place_ref[0] * part, part) for k in range(4)]
            left = jnp.concatenate([rows0[pl.ds(at, part), :] for at in starts], axis=0)
            right = jnp.concatenate([rows1[pl.ds(at, part), :] for at in starts], axis=0)
            term = jnp.dot(left, q0[...], preferred_element_type=F32)
            term = (term + jnp.dot(right, q1[...], preferred_element_type=F32)).astype(BF)
            pieces = []
            for k in range(4):
                own = term[k * part : (k + 1) * part]
                pieces += [own[:, :tile], own[:, tile:]]
            store(0, jnp.concatenate(pieces, axis=0))

        @pl.when(j == 1)
        def _():
            finish(tile, g0, g1)

        @pl.when(j == 2)
        def _():
            finish(tile + half, u0, u1)

    def fixed(shape):
        return pl.BlockSpec(shape, lambda j, place_ref: (0, 0))

    own_half = pl.BlockSpec((width, half), lambda j, place_ref: (0, place_ref[0]))
    taken = pl.BlockSpec((chunks, rows_each, width), lambda j, place_ref: (0, 0, 0))
    in_specs = [
        taken,
        taken,
        fixed((width, 2 * tile)),
        fixed((width, 2 * tile)),
        own_half,
        fixed((width, half)),
        own_half,
        fixed((width, half)),
    ]
    return pl.pallas_call(
        kernel,
        grid_spec=pltpu.PrefetchScalarGridSpec(
            num_scalar_prefetch=1,
            grid=(3,),
            in_specs=in_specs + after(deps),
            out_specs=[fixed((n * part, tile + 2 * half)) for n in (2, 1, 1, 2, 2)],
            scratch_shapes=[pltpu.VMEM((count, width), BF)] * 2,
        ),
        out_shape=[jax.ShapeDtypeStruct((n * part, tile + 2 * half), BF) for n in (2, 1, 1, 2, 2)],
        compiler_params=pltpu.CompilerParams(
            dimension_semantics=("arbitrary",), vmem_limit_bytes=BIG
        ),
        cost_estimate=cost(11),
        name=name,
    )(place, *toks, *wqs, *gates, *ups, *deps)


def middle(bottom, top, from_left, from_right, deps, name):
    r, whole_width = top.shape

    def body(bottom_ref, top_ref, left_ref, right_ref, up_ref, down_ref):
        up_ref[...] = (
            bottom_ref[...].astype(F32) + left_ref[r : 2 * r].astype(F32)
        ).astype(BF)
        down_ref[...] = (top_ref[...].astype(F32) + right_ref[0:r].astype(F32)).astype(BF)

    shape = jax.ShapeDtypeStruct((r, whole_width), BF)
    return simple_call(body, [shape, shape], [bottom, top, from_left, from_right], deps, name)


def tail(low, from_left, from_right, left_sum, right_sum, deps, name):
    r, whole_width = left_sum.shape

    def body(low_ref, left_ref, right_ref, ls_ref, rs_ref, out_ref):
        out_ref[0:r] = (
            low_ref[0:r].astype(F32) + right_ref[r : 2 * r].astype(F32) + ls_ref[...].astype(F32)
        ).astype(BF)
        out_ref[r : 2 * r] = (
            low_ref[r : 2 * r].astype(F32) + left_ref[0:r].astype(F32) + rs_ref[...].astype(F32)
        ).astype(BF)

    shape = jax.ShapeDtypeStruct((2 * r, whole_width), BF)
    return simple_call(
        body, shape, [low, from_left, from_right, left_sum, right_sum], deps, name
    )


def gate_all(values, deps):
    count = len(values)

    def kernel(*refs):
        pass

    return pl.pallas_call(
        kernel,
        in_specs=after(values) + after(deps),
        out_specs=after(values),
        out_shape=[jax.ShapeDtypeStruct(value.shape, value.dtype) for value in values],
        input_output_aliases={k: k for k in range(count)},
        cost_estimate=NO_COST,
        name="gate",
    )(*values, *deps)


def gate(value, deps):
    return gate_all([value], deps)[0]


def branches(own, other, kv_one, kv_two, key_pos, pos, query_pos, cosine, sine, deps, name):
    rows, total = own.shape
    part = rows // 2
    head = 2 * cosine.shape[1]
    tile = 3 * head // 2
    heads = 2 * tile // head
    each = (total // tile - 1) // 2

    def body(own_ref, oth_ref, one_ref, two_ref, kp_ref, pos_ref, qp_ref, cos_ref, sin_ref, out_ref):
        key_position = kp_ref[0:1, :]
        pack = jnp.concatenate([one_ref[:, 2 * head :], two_ref[:, 2 * head :]], axis=0)

        def scale_of(position):
            onehot = (position == key_position).astype(F32).astype(BF)
            parts = jnp.dot(onehot, pack, preferred_element_type=F32)
            return parts[:, 0:1] + parts[:, 1:2] + parts[:, 2:3]

        def block(k, start, size):
            at = (slice(start, start + size), slice(k * tile, (k + 1) * tile))
            return own_ref[at].astype(F32) + oth_ref[at].astype(F32)

        position = qp_ref[:, 0:1]
        raw = jnp.concatenate([block(0, 0, part), block(0, part, part)], axis=1)
        raw = scale_of(position) * raw
        cos, sin = cos_ref[...], sin_ref[...]
        queries = jnp.concatenate(
            [turn(raw[:, k * head : (k + 1) * head], cos, sin) for k in range(heads)], axis=0
        ).astype(BF)
        keys = jnp.concatenate([one_ref[:, :head], two_ref[:, :head]], axis=0)
        values = jnp.concatenate(
            [one_ref[:, head : 2 * head], two_ref[:, head : 2 * head]], axis=0
        )
        scores = lax.dot_general(
            queries, keys, (((1,), (1,)), ((), ())), preferred_element_type=F32
        ) * float(head) ** (-0.5)
        allowed = jnp.where(position >= key_position, 1.0, 0.0)
        allowed = jnp.concatenate([allowed] * heads, axis=0)
        scores = jnp.where(allowed > 0.5, scores, -1e30)
        expo = jnp.exp(scores - jnp.max(scores, axis=1, keepdims=True))
        weights = (expo / jnp.sum(expo, axis=1, keepdims=True)).astype(BF)
        attended = jnp.dot(weights, values, preferred_element_type=F32)
        attended = jnp.concatenate(
            [attended[k * part : (k + 1) * part] for k in range(heads)], axis=1
        ).astype(BF)
        out_ref[0:part, 0:tile] = attended[:, :tile]
        out_ref[part:rows, 0:tile] = attended[:, tile:]
        scale = scale_of(pos_ref[:, 0:1])
        for k in range(1, each + 1):
            gate_part = scale * block(k, 0, rows)
            up_part = scale * block(each + k, 0, rows)
            out_ref[:, k * tile : (k + 1) * tile] = (
                gate_part / (1.0 + jnp.exp(-gate_part)) * up_part
            ).astype(BF)

    return simple_call(
        body,
        jax.ShapeDtypeStruct((rows, (each + 1) * tile), BF),
        [own, other, kv_one, kv_two, key_pos, pos, query_pos, cosine, sine],
        deps,
        name,
        3,
    )


def project_out(place, mine, theirs, wo, w_down, paired, deps, name, time):
    group, depth = mine[0].shape
    count = 4 * group
    part = group // 2
    width = wo.shape[1]
    tile = wo.shape[0] // 2
    half = depth - tile
    each = group // 4

    def kernel(place_ref, *refs):
        m_refs, t_refs, (wo_ref, wd_ref) = refs[0:4], refs[4:8], refs[8:10]
        *out_refs, total, attended, hidden = refs[10 + len(deps) :]
        k = pl.program_id(0)

        @pl.when(k == 0)
        def _():
            for refs_of, core in ((m_refs, place_ref[0]), (t_refs, 1 - place_ref[0])):
                for g, ref in enumerate(refs_of):
                    at = pl.multiple_of(g * group + core * part, part)
                    for side in range(2):
                        attended[pl.ds(at, part), side * tile : (side + 1) * tile] = ref[
                            side * part : (side + 1) * part, 0:tile
                        ]
            for g, ref in enumerate(m_refs):
                hidden[g * group : (g + 1) * group, :] = ref[:, tile:]
            total[...] = jnp.dot(attended[...], wo_ref[...], preferred_element_type=F32)

        @pl.when(k == 1)
        def _():
            total[...] += jnp.dot(hidden[...], wd_ref[...], preferred_element_type=F32)
            for g, ref in enumerate(t_refs):
                hidden[g * group : (g + 1) * group, :] = ref[:, tile:]

        @pl.when(k == 2)
        def _():
            total[...] += jnp.dot(hidden[...], wd_ref[...], preferred_element_type=F32)
            mine_yl = place_ref[2]
            for g in range(4):
                absolute = lax.rem(place_ref[1] + g, 4)
                if not paired:
                    for chunk in range(4):
                        start = g * group + chunk * each
                        out_refs[0][absolute * 4 + chunk] = total[start : start + each].astype(BF)
                    continue
                for side in range(2):
                    start = g * group + side * 2 * each
                    own = pl.ds(pl.multiple_of(start + mine_yl * each, each), each)
                    other = pl.ds(pl.multiple_of(start + (1 - mine_yl) * each, each), each)
                    out_refs[0][absolute * 2 + side] = total[own, :]
                    out_refs[1][absolute * 2 + side] = total[other, :].astype(BF)

    def fixed(shape):
        return pl.BlockSpec(shape, lambda k, place_ref: (0, 0))

    if paired:
        out_shape = [jax.ShapeDtypeStruct((8, each, width), kind) for kind in (F32, BF)]
    else:
        out_shape = [jax.ShapeDtypeStruct((16, each, width), BF)]

    def down_at(k, place_ref):
        return (jnp.where(k < 2, place_ref[0], 1 - place_ref[0]), 0)

    return pl.pallas_call(
        kernel,
        grid_spec=pltpu.PrefetchScalarGridSpec(
            num_scalar_prefetch=1,
            grid=(3,),
            in_specs=[
                *[fixed((group, depth))] * 8,
                fixed((2 * tile, width)),
                pl.BlockSpec((half, width), down_at),
            ]
            + after(deps),
            out_specs=[
                pl.BlockSpec(shape.shape, lambda k, place_ref: (0, 0, 0)) for shape in out_shape
            ],
            scratch_shapes=[
                pltpu.VMEM((count, width), F32),
                pltpu.VMEM((count, 2 * tile), BF),
                pltpu.VMEM((count, half), BF),
            ],
        ),
        out_shape=out_shape,
        compiler_params=pltpu.CompilerParams(
            dimension_semantics=("arbitrary",), vmem_limit_bytes=BIG
        ),
        cost_estimate=cost(time),
        name=name,
    )(place, *mine, *theirs, wo, w_down, *deps)


def on_device(tokens, gain, wq, wkv, w_gate, w_up, wo, w_down):
    b = lax.axis_index("blk")
    t = lax.axis_index("batch")
    x, c = (b // 2) % 4, b % 2
    place = jnp.stack([c, x, t % 2]).astype(jnp.int32)
    rows, width = tokens.shape
    features = width * 16
    seq = rows * 16
    nq = wq.shape[1]
    head = wkv.shape[1] // 2
    half_rows = rows // 2

    tokens_f = tokens.astype(F32)
    scaled = (tokens_f * gain.astype(F32)).astype(BF)

    part = w_gate.shape[1] // 2
    wqs = (wq, blk_send(wq, dc=1))
    gates, ups = tuple(
        (w, blk_send(lax.dynamic_slice_in_dim(w, (1 - c) * part, part, 1), dc=1))
        for w in (w_gate, w_up)
    )

    starts = [sum(STAGES[:k]) for k in range(len(STAGES))]

    def spread_rows(value):
        return jnp.broadcast_to(value[None], (16,) + value.shape)

    def to_all(value):
        return lax.all_to_all(value, "batch", 0, 0)

    def position_of(k, index):
        return (index // STAGES[k]) * rows + starts[k] + index % STAGES[k]

    def wide(position):
        return jnp.broadcast_to(position[:, None], (position.shape[0], 128)).astype(jnp.int32)

    places = []
    for k, count in enumerate(STAGES):
        group = 16 * count // 4
        position = position_of(k, x * group + jnp.arange(group))
        query_at = position_of(k, x * group + c * (group // 2) + jnp.arange(group // 2))
        places.append((wide(position), wide(query_at), *angles(query_at, head // 2)))

    squares = jnp.sum(tokens_f * tokens_f, axis=1, keepdims=True)
    kv_part = jnp.dot(scaled, wkv, preferred_element_type=F32)
    payload = jnp.concatenate([kv_part, jnp.broadcast_to(squares, (rows, 128))], axis=1)
    kv_keep = lax.dynamic_slice_in_dim(payload, c * half_rows, half_rows, 0)
    kv_give = lax.dynamic_slice_in_dim(payload, (1 - c) * half_rows, half_rows, 0)
    kv_got = blk_send(kv_give, dc=1)

    kv_sum = kv_keep + kv_got
    kv_sum = kv_sum + blk_send(kv_sum, xor=1)
    kv_sum = kv_sum + blk_send(kv_sum, xor=2)

    def term_of(tok, deps):
        return project(place, (tok, blk_send(tok, dc=1)), wqs, gates, ups, deps, "term")

    def own_rows(k):
        return scaled[starts[k] : starts[k] + STAGES[k]]

    def step_one(term):
        return blk_send(term[3], dx=1), blk_send(term[4], dx=-1)

    def step_two(sums):
        return blk_send(sums[0], dx=1), blk_send(sums[1], dx=-1)

    tok_1 = gate(to_all(spread_rows(own_rows(0))), [kv_sum])
    tok_2 = to_all(gate(spread_rows(own_rows(1)), [tok_1]))
    term_1 = term_of(tok_1, [])
    one_1 = step_one(term_1)
    kv_half = gate(kv_sum, [term_1[0]])
    kv_sum = kv_half + blk_send(kv_half, dyh=1)
    tok_2 = gate(tok_2, [kv_sum])
    row_scale = lax.rsqrt(kv_sum[:, 2 * head : 2 * head + 1] / features + 1e-06)
    own_cos, own_sin = angles(t * rows + c * half_rows + jnp.arange(half_rows), head // 2)
    key_own = turn(row_scale * kv_sum[:, :head], own_cos, own_sin).astype(BF)
    value_own = (row_scale * kv_sum[:, head : 2 * head]).astype(BF)
    scale_hi = lax.reduce_precision(row_scale, 8, 7)
    scale_mid = lax.reduce_precision(row_scale - scale_hi, 8, 7)
    scale_lo = row_scale - scale_hi - scale_mid
    lane = lax.broadcasted_iota(jnp.int32, (half_rows, 128), 1)
    scale_cols = jnp.where(
        lane == 0, scale_hi, jnp.where(lane == 1, scale_mid, jnp.where(lane == 2, scale_lo, 0.0))
    ).astype(BF)
    kv_own = jnp.concatenate([key_own, value_own, scale_cols], axis=1)
    kv_own = gate(spread_rows(kv_own), [tok_2])
    mid_1 = middle(term_1[1], term_1[2], *one_1, [kv_own], "mid")
    two_1 = step_two(mid_1)
    term_2 = term_of(tok_2, [])
    one_2 = step_one(term_2)
    own_1 = tail(term_1[0], *one_1, *two_1, [], "tail")
    mid_2 = middle(term_2[1], term_2[2], *one_2, [own_1], "mid")
    two_2 = step_two(mid_2)

    kv_one = to_all(kv_own).reshape(seq // 2, -1)
    kv_two = blk_send(kv_one, dc=1)
    at = jnp.arange(seq)
    side = jnp.where(at < seq // 2, c, 1 - c)
    at = at % (seq // 2)
    key_pos = (at // half_rows) * rows + side * half_rows + at % half_rows
    key_pos = jnp.broadcast_to(key_pos[None, :], (8, seq)).astype(jnp.int32)

    def branch_of(s, own, deps, name):
        other = blk_send(own, dyh=1)
        return branches(own, other, kv_one, kv_two, key_pos, *places[s], deps, name)

    def spread(branch):
        return [blk_send(branch, dx=-k) for k in (1, 2, 3)]

    def collect(branch, others):
        mine = [branch, *others]
        return mine, [blk_send(piece, dc=1) for piece in mine]

    def pair_sum(out):
        pairs = [(k, k ^ 1) for k in range(16)]
        return (out[0] + lax.ppermute(out[1], "batch", pairs).astype(F32)).astype(BF)

    branch_1 = branch_of(0, own_1, [mid_2[0]], "branch")
    spread_1 = spread(branch_1)
    own_2 = tail(term_2[0], *one_2, *two_2, [branch_1], "tail")
    branch_2 = branch_of(1, own_2, [], "branch")
    spread_2 = spread(branch_2)
    out_1 = project_out(place, *collect(branch_1, spread_1), wo, w_down, True, [branch_2], "out", 8)
    spread_2 = gate_all(spread_2, [out_1[0]])
    pair_1 = pair_sum(out_1)
    out_2 = project_out(
        place, *collect(branch_2, spread_2), wo, w_down, False, [pair_1], "out", 8
    )
    part_1 = lax.all_to_all(pair_1, "batch", 0, 0, axis_index_groups=Z_GROUPS)
    part_2 = lax.all_to_all(out_2[0], "batch", 0, 0)
    sums = [jnp.sum(part.astype(F32), axis=0) for part in (part_1, part_2)]
    return tokens_f + jnp.concatenate(sums, axis=0)


def solution(mesh):
    in_specs = (
        P("batch", "blk"),
        P("blk"),
        P("blk", "batch"),
        P("blk", None),
        P("blk", "batch"),
        P("blk", "batch"),
        P("batch", "blk"),
        P("batch", "blk"),
    )
    out_specs = P("batch", "blk")
    return jax.shard_map(
        on_device, mesh=mesh, in_specs=in_specs, out_specs=out_specs, check_vma=False
    )
```
